32 devices in a mesh: dp: 4 (over z), row: 4 (over x, core), col: 2 (over y).
Axes of the slice: x: 2, y: 2, z: 4, core: 2. Of those that a mesh axis runs over, the one named last changes fastest.
Arguments:
- layer_input: bfloat16 [16384, 768], P(('dp', 'row')), may hold values from -6 to 6
- norm_gain: float32 [768], replicated, may hold values from 0.5 to 1.5
- gate_weight: bfloat16 [768, 1536], P('row', 'col'), may hold values from -0.21875 to 0.21875
- value_weight: bfloat16 [768, 1536], P('row', 'col'), may hold values from -0.21875 to 0.21875
- state_weight: bfloat16 [768, 256], P('row'), may hold values from -0.21875 to 0.21875
- step_weight: bfloat16 [768, 24], P('row', 'col'), may hold values from -0.21875 to 0.21875
- value_kernel: float32 [4, 1536], P(None, 'col'), may hold values from -3 to 3
- value_bias: float32 [1536], P('col'), may hold values from -1.5 to 1.5
- state_kernel: float32 [4, 256], replicated, may hold values from -3 to 3
- state_bias: float32 [256], replicated, may hold values from -1.5 to 1.5
- step_bias: float32 [24], P('col'), may hold values from -5 to -2.5
- decay_log: float32 [24], P('col'), may hold values from -7 to 0.5
- skip_gain: float32 [24], P('col'), may hold values from 0.5 to 1.5
- gate_gain: float32 [1536], P('col'), may hold values from 0.5 to 1.5
- out_weight: bfloat16 [768, 1536], P('row', 'col'), may hold values from -0.15625 to 0.15625
- out_grad: bfloat16 [16384, 768], P(('dp', 'row')), may hold values from -6 to 6
Outputs:
- mixed_out: bfloat16 [16384, 768], P(('dp', 'row'))
- input_grad: float32 [16384, 768], P(('dp', 'row'))
- norm_gain_grad: float32 [768], replicated
- gate_weight_grad: float32 [768, 1536], P('row', 'col')
- value_weight_grad: float32 [768, 1536], P('row', 'col')
- state_weight_grad: float32 [768, 256], P('row')
- step_weight_grad: float32 [768, 24], P('row', 'col')
- value_kernel_grad: float32 [4, 1536], P(None, 'col')
- value_bias_grad: float32 [1536], P('col')
- state_kernel_grad: float32 [4, 256], replicated
- state_bias_grad: float32 [256], replicated
- step_bias_grad: float32 [24], P('col')
- decay_log_grad: float32 [24], P('col')
- skip_gain_grad: float32 [24], P('col')
- gate_gain_grad: float32 [1536], P('col')
- out_weight_grad: float32 [768, 1536], P('row', 'col')
The draws below stay inside these ranges and needn't reach their ends.
All inputs are finite; a program needn't handle non-finite values.
Results may differ from the reference program's by a relative error of at most 0.00155.
The reference program's roundings to bfloat16 on the way count: a program that leaves them out, or rounds other values in their place, can miss the bound.
Values may be sent and summed in bfloat16 or wider, within the bound.
A program may use at most 192 MiB of HBM per device.

```python
import jax
import jax.numpy as jnp
from jax import lax

D = 768
HEADS = 24
HEADDIM = 64
STATE = 128
CONV = 4
SPAN = 256
SEQ_LEN = 4096
INNER = 1536
TOKENS = 16384
N_COL = 2


def with_spikes(result, stream_key, source, target, blocks, factor):
    owner, partner = [(jnp.arange(result.shape[dim]) // (result.shape[dim] // blocks)).reshape([-1 if axis == dim else 1 for axis in range(result.ndim)]) for dim in (source, target)]
    chosen = jax.random.permutation(stream_key, blocks)[partner]
    strong = (owner == chosen) | (owner == (partner + blocks // 2) % blocks)
    return jnp.where(strong, factor * result, result)


def levels(stream_key, extent, split, low, high):
    level, own = 1.0, jax.random.fold_in(stream_key, 6)
    for axis_at, blocks in split:
        steps = jnp.exp(jax.random.uniform(jax.random.fold_in(own, axis_at), (blocks,), jnp.float32, low / len(split), high / len(split)))
        level = level * jnp.repeat(steps, extent[axis_at] // blocks).reshape([-1 if axis == axis_at else 1 for axis in range(len(extent))])
    return level


def gaussian(rng, shape, deviation, bound, cuts=(), kind=jnp.bfloat16):
    gain = levels(rng, shape, cuts, -0.22, 0.18) if cuts else 1.0
    entries = jax.random.normal(rng, shape, jnp.float32) * deviation * gain
    return jnp.minimum(jnp.maximum(entries, -bound), bound).astype(kind)


def noise_with(rng, extent, deviation, limit, cuts, heavy, kind=jnp.bfloat16):
    drawn = deviation * jax.random.normal(rng, extent, jnp.float32)
    if cuts:
        drawn = drawn * levels(rng, extent, cuts, -0.22, 0.18)
    return jnp.clip(with_spikes(drawn, jax.random.fold_in(rng, 3), *heavy), -limit, limit).astype(kind)


def setup_inputs(seed: int = 0) -> dict:
    key_of = jax.random.split(jax.random.key(seed), 17)
    layer_input = gaussian(key_of[0], (TOKENS, D), 1.0, 6.0, ((0, 16),))
    norm_gain = jnp.clip(1.0 + 0.1 * jax.random.normal(key_of[1], (D,), jnp.float32), 0.5, 1.5)
    gate_weight = gaussian(key_of[2], (D, INNER), D ** -0.5, 0.21875, ((0, 4), (1, 2)))
    value_weight = gaussian(key_of[3], (D, INNER), D ** -0.5, 0.21875, ((0, 4), (1, 2)))
    state_weight = gaussian(key_of[4], (D, 2 * STATE), D ** -0.5, 0.21875, ((0, 4),))
    step_weight = gaussian(key_of[5], (D, HEADS), D ** -0.5, 0.21875, ((0, 4), (1, 2)))
    value_kernel = gaussian(key_of[6], (CONV, INNER), CONV ** -0.5, 3.0, ((1, 2),), jnp.float32)
    value_bias = gaussian(key_of[7], (INNER,), 0.3, 1.5, ((0, 2),), jnp.float32)
    state_kernel = gaussian(key_of[8], (CONV, 2 * STATE), CONV ** -0.5, 3.0, (), jnp.float32)
    state_bias = gaussian(key_of[9], (2 * STATE,), 0.3, 1.5, (), jnp.float32)
    step_bias = jnp.clip(-5.0 + 2.5 * jax.random.uniform(key_of[10], (HEADS,), jnp.float32) ** levels(key_of[10], (HEADS,), ((0, 2),), -0.2, 0.2), -5.0, -2.5)
    decay_log = jnp.clip(-7.0 + 7.5 * jax.random.uniform(key_of[11], (HEADS,), jnp.float32) ** levels(key_of[11], (HEADS,), ((0, 2),), -0.2, 0.2), -7.0, 0.5)
    skip_gain = jnp.clip(0.5 + 1.0 * jax.random.uniform(key_of[12], (HEADS,), jnp.float32) ** levels(key_of[12], (HEADS,), ((0, 2),), -0.2, 0.2), 0.5, 1.5)
    gate_gain = jnp.clip(1.0 + 0.1 * jax.random.normal(key_of[13], (INNER,), jnp.float32), 0.5, 1.5)
    out_weight = gaussian(key_of[14], (D, INNER), INNER ** -0.5, 0.15625, ((0, 4), (1, 2)))
    out_grad = noise_with(key_of[15], (TOKENS, D), 1.0, 6.0, ((0, 16),), (0, 1, 16, 2.0))
    return dict(layer_input=layer_input, norm_gain=norm_gain, gate_weight=gate_weight, value_weight=value_weight, state_weight=state_weight, step_weight=step_weight, value_kernel=value_kernel, value_bias=value_bias, state_kernel=state_kernel, state_bias=state_bias, step_bias=step_bias, decay_log=decay_log, skip_gain=skip_gain, gate_gain=gate_gain, out_weight=out_weight, out_grad=out_grad)


EPSILON = 1e-05
HIGHEST = lax.Precision.HIGHEST

@jax.custom_vjp
def low(v):
    return lax.optimization_barrier(v.astype(jnp.bfloat16)).astype(jnp.float32)

@jax.custom_vjp
def low_back(v):
    return v

def low_keep(v):
    return (low(v), None)

def low_pass(kept, grad):
    return (grad,)

def back_keep(v):
    return (v, None)

def back_low(kept, grad):
    return (low(grad),)
low.defvjp(low_keep, low_pass)
low_back.defvjp(back_keep, back_low)

def rms_scale(values):
    return lax.rsqrt(lax.optimization_barrier(jnp.mean(values * values, axis=-1, keepdims=True)) + EPSILON)

def conv_silu(before, kernel, kernel_bias, margin_rows):
    extended = jnp.concatenate([margin_rows, before], axis=0)
    amount = before.shape[0]
    tap_count = kernel.shape[0]
    summed = kernel_bias[None, :] + sum((kernel[tap_index][None, :] * extended[tap_index:tap_index + amount] for tap_index in range(tap_count)))
    return jax.nn.silu(summed)

def span_step(carried_in, block_data):
    carry_state, offset = carried_in
    x_heads, step_size, log_decay, b_input, c_output = block_data
    length = x_heads.shape[0]
    cumulative = jnp.cumsum(log_decay, axis=0)
    by_head = cumulative.T
    differences = by_head[:, :, None] - by_head[:, None, :]
    row_ids = lax.broadcasted_iota(jnp.int32, (length, length), 0)
    col_ids = lax.broadcasted_iota(jnp.int32, (length, length), 1)
    causal = (row_ids >= col_ids)[None]
    decays = jnp.where(causal, jnp.exp(jnp.where(causal, differences, 0.0)), 0.0)
    inner_gram = jnp.dot(c_output, b_input.T, precision=HIGHEST)
    weights = decays * inner_gram[None]
    x_scaled = x_heads * step_size[:, :, None]
    within = jnp.einsum('hts,shp->thp', weights, x_scaled, precision=HIGHEST)
    carried = jnp.einsum('tn,hpn->thp', c_output, carry_state, precision=HIGHEST)
    y_heads = within + jnp.exp(cumulative)[:, :, None] * carried
    final_cum = cumulative[-1]
    to_end = jnp.exp(final_cum[None, :] - cumulative)
    new_state = jnp.exp(final_cum)[:, None, None] * carry_state + jnp.einsum('sh,shp,sn->hpn', to_end, x_scaled, b_input, precision=HIGHEST)
    return ((new_state, offset + final_cum), (y_heads, offset[None, :] + cumulative))

def span_scan(x_heads, step_size, log_decay, b_input, c_output):
    amount, head_part, head_width = x_heads.shape
    blocks = amount // SPAN
    carry_state = jnp.zeros((head_part, head_width, b_input.shape[1]), x_heads.dtype)
    offset = jnp.zeros((head_part,), x_heads.dtype)
    shaped = (x_heads.reshape(blocks, SPAN, head_part, head_width), step_size.reshape(blocks, SPAN, head_part), log_decay.reshape(blocks, SPAN, head_part), b_input.reshape(blocks, SPAN, -1), c_output.reshape(blocks, SPAN, -1))
    (end_state, total_log), (y_heads, cumulative) = lax.scan(jax.checkpoint(span_step), (carry_state, offset), shaped)
    return (y_heads.reshape(amount, head_part, head_width), end_state, total_log, cumulative.reshape(amount, head_part))

def layer(layer_rows, norm_gain, gate_weight, value_weight, state_weight, step_weight, value_kernel, value_bias, state_kernel, state_bias, step_bias, decay_log, skip_gain, gate_gain, out_weight):
    normed = low(layer_rows * rms_scale(layer_rows) * norm_gain)
    gate_pre = low_back(jnp.dot(normed, gate_weight, precision=HIGHEST))
    value_pre = low_back(jnp.dot(normed, value_weight, precision=HIGHEST))
    step_pre = low_back(jnp.dot(normed, step_weight, precision=HIGHEST))
    state_pre = jnp.dot(normed, state_weight, precision=HIGHEST)
    amount = layer_rows.shape[0]
    margin = CONV - 1
    x_conv = conv_silu(value_pre, value_kernel, value_bias, jnp.zeros((margin, value_pre.shape[1]), layer_rows.dtype))
    step_size = jax.nn.softplus(step_pre + step_bias)
    log_decay = -step_size * jnp.exp(decay_log)
    head_part = HEADS // N_COL
    group_width = head_part * HEADDIM
    pieces = []
    for column_group in range(N_COL):
        state_copy = low_back(state_pre)
        bc_conv = conv_silu(state_copy, state_kernel, state_bias, jnp.zeros((margin, state_pre.shape[1]), layer_rows.dtype))
        heads_from = column_group * head_part
        x_heads = x_conv[:, column_group * group_width:(column_group + 1) * group_width].reshape(amount, head_part, HEADDIM)
        y_heads, end_state, total_log, cumulative = span_scan(x_heads, step_size[:, heads_from:heads_from + head_part], log_decay[:, heads_from:heads_from + head_part], bc_conv[:, :STATE], bc_conv[:, STATE:])
        y_heads = y_heads + skip_gain[heads_from:heads_from + head_part][None, :, None] * x_heads
        pieces.append(y_heads.reshape(amount, group_width))
    y_flat = jnp.concatenate(pieces, axis=1)
    gated = y_flat * jax.nn.silu(gate_pre)
    mixed_low = low(gated * rms_scale(gated) * gate_gain)
    return layer_rows + jnp.dot(mixed_low, out_weight.T, precision=HIGHEST)

def reference(layer_input, norm_gain, gate_weight, value_weight, state_weight, step_weight, value_kernel, value_bias, state_kernel, state_bias, step_bias, decay_log, skip_gain, gate_gain, out_weight, out_grad):
    params = tuple((tensor.astype(jnp.float32) for tensor in (norm_gain, gate_weight, value_weight, state_weight, step_weight, value_kernel, value_bias, state_kernel, state_bias, step_bias, decay_log, skip_gain, gate_gain, out_weight)))
    sequences = TOKENS // SEQ_LEN
    inputs = layer_input.astype(jnp.float32).reshape(sequences, SEQ_LEN, D)
    cotangent_rows = out_grad.astype(jnp.float32).reshape(sequences, SEQ_LEN, D)

    def one_sequence(running, paired):
        seq_rows, seq_grad = paired
        outcome, pullback = jax.vjp(layer, seq_rows, *params)
        cotangents = pullback(seq_grad)
        running = tuple((summed + addend for summed, addend in zip(running, cotangents[1:])))
        return (running, (outcome.astype(jnp.bfloat16), cotangents[0]))
    initial = tuple((jnp.zeros_like(tensor) for tensor in params))
    totals, (outputs, input_grads) = lax.scan(one_sequence, initial, (inputs, cotangent_rows))
    return (outputs.reshape(TOKENS, D), input_grads.reshape(TOKENS, D), totals[0], totals[1], totals[2], totals[3], totals[4], totals[5], totals[6], totals[7], totals[8], totals[9], totals[10], totals[11], totals[12], totals[13])
```

```python
import functools

import jax
import jax.numpy as jnp
from jax import lax
from jax.experimental import pallas as pl
from jax.experimental.pallas import tpu as pltpu
from jax.sharding import PartitionSpec as P

D = 768
HEADDIM = 64
STATE = 128
CONV = 4
SPAN = 256
INNER = 1536


EPSILON = 1e-05
HIGHEST = lax.Precision.HIGHEST


def from_behind(x, axis, by):
    peers = lax.axis_size(axis)
    pairs = [(i, i + by) for i in range(peers) if 0 <= i + by < peers]
    return lax.ppermute(x, axis, pairs)


def entering(value, axis, join, neutral, backward):
    count, mine = (lax.axis_size(axis), lax.axis_index(axis))
    pieces = jax.tree.map(lambda part: lax.all_gather(part, axis), value)
    if backward:
        pieces = jax.tree.map(lambda part: part[::-1], pieces)
        mine = count - 1 - mine
    total = jax.tree.map(
        lambda part, zero: jnp.full_like(part, 0) + jnp.asarray(zero, part.dtype), value, neutral
    )

    def turn(position, total):
        longer = join(total, jax.tree.map(lambda part: part[position], pieces))
        return jax.tree.map(lambda new, old: jnp.where(position < mine, new, old), longer, total)

    return lax.fori_loop(0, count - 1, turn, total)


def rms_scale(values):
    return lax.rsqrt(jnp.mean(values * values, axis=-1, keepdims=True) + EPSILON)


def conv_silu(before, kernel, kernel_bias, margin_rows):
    extended = jnp.concatenate([margin_rows, before], axis=0)
    amount = before.shape[0]
    tap_count = kernel.shape[0]
    summed = kernel_bias[None, :] + sum(
        (
            kernel[tap_index][None, :] * extended[tap_index : tap_index + amount]
            for tap_index in range(tap_count)
        )
    )
    return jax.nn.silu(summed)


NN = (((1,), (0,)), ((), ()))
NT = (((1,), (1,)), ((), ()))
TN = (((0,), (0,)), ((), ()))


def split(v):
    high = v.astype(jnp.bfloat16)
    return high, (v - high.astype(jnp.float32)).astype(jnp.bfloat16)


def dot3(a, b, dims):
    def product(u, v):
        return lax.dot_general(u, v, dims, preferred_element_type=jnp.float32)

    return product(a[0], b[0]) + (product(a[0], b[1]) + product(a[1], b[0]))


def ones_dot(ones, v):
    first, second = split(v)
    third = (v - first.astype(jnp.float32) - second.astype(jnp.float32)).astype(jnp.bfloat16)

    def product(u):
        return lax.dot_general(ones, u, NN, preferred_element_type=jnp.float32)

    return product(first) + (product(second) + product(third))


def spread(per_head, pair, width):
    rows = per_head.shape[0]
    lane = lax.broadcasted_iota(jnp.int32, (rows, width), 1)
    low = jnp.broadcast_to(per_head[:, 2 * pair : 2 * pair + 1], (rows, width))
    high = jnp.broadcast_to(per_head[:, 2 * pair + 1 : 2 * pair + 2], (rows, width))
    return jnp.where(lane < HEADDIM, low, high)


def spread_all(per_head, heads):
    return jnp.concatenate([spread(per_head, j, 2 * HEADDIM) for j in range(heads // 2)], axis=1)


def decay_state(state, factor, heads):
    return jnp.concatenate(
        [state[h * HEADDIM : (h + 1) * HEADDIM] * factor[:, h : h + 1] for h in range(heads)],
        axis=0,
    )


def triangle(lower):
    rows = lax.broadcasted_iota(jnp.int32, (SPAN, SPAN), 0)
    cols = lax.broadcasted_iota(jnp.int32, (SPAN, SPAN), 1)
    return rows >= cols if lower else rows <= cols


def end_state_kernel(heads, x_ref, dt_ref, ld_ref, bc_ref, cum_ref, end_ref):
    @pl.when(pl.program_id(0) == 0)
    def _():
        end_ref[...] = jnp.zeros_like(end_ref)

    ones = triangle(True).astype(jnp.bfloat16)
    cum = ones_dot(ones, ld_ref[...])
    cum_ref[...] = cum
    final = cum[SPAN - 1 : SPAN]
    weighted = x_ref[...] * spread_all(dt_ref[...] * jnp.exp(final - cum), heads)
    added = dot3(split(weighted), split(bc_ref[:, :STATE]), TN)
    end_ref[...] = decay_state(end_ref[...], jnp.exp(final), heads) + added


def forward_kernel(heads, x_ref, dt_ref, cum_ref, cumt_ref, bc_ref, entry_ref, y_ref, s_ref, state):
    @pl.when(pl.program_id(0) == 0)
    def _():
        state[...] = entry_ref[...]

    cum = cum_ref[...]
    final = cum[SPAN - 1 : SPAN]
    b_low = split(bc_ref[:, :STATE])
    c_low = split(bc_ref[:, STATE:])
    gram = dot3(c_low, b_low, NT)
    carry = state[...]
    s_ref[0] = carry
    carried = dot3(c_low, split(carry), NT)
    causal = triangle(True)
    lane = lax.broadcasted_iota(jnp.int32, (SPAN, 2 * HEADDIM), 1)
    to_end = jnp.exp(final - cum)
    grown = jnp.exp(cum)
    weighted = []
    for j in range(heads // 2):
        at = slice(2 * HEADDIM * j, 2 * HEADDIM * (j + 1))
        xs = x_ref[:, at] * spread(dt_ref[...], j, 2 * HEADDIM)
        xs_low = split(xs)
        parts = []
        for h in (2 * j, 2 * j + 1):
            gap = cum[:, h : h + 1] - cumt_ref[h : h + 1, :]
            decay = jnp.exp(jnp.where(causal, gap, -1e30))
            parts.append(dot3(split(decay * gram), xs_low, NN))
        within = jnp.where(lane < HEADDIM, parts[0], parts[1])
        y_ref[:, at] = within + spread(grown, j, 2 * HEADDIM) * carried[:, at]
        weighted.append(xs * spread(to_end, j, 2 * HEADDIM))
    added = dot3(split(jnp.concatenate(weighted, axis=1)), b_low, TN)
    state[...] = decay_state(carry, jnp.exp(final), heads) + added


def entry_grad_kernel(heads, dy_ref, cum_ref, bc_ref, out_ref):
    @pl.when(pl.program_id(0) == 0)
    def _():
        out_ref[...] = jnp.zeros_like(out_ref)

    cum = cum_ref[...]
    grown = dy_ref[...] * spread_all(jnp.exp(cum), heads)
    added = dot3(split(grown), split(bc_ref[:, STATE:]), TN)
    out_ref[...] = decay_state(out_ref[...], jnp.exp(cum[SPAN - 1 : SPAN]), heads) + added


def backward_kernel(
    heads, x_ref, dt_ref, cum_ref, cumt_ref, bc_ref, dy_ref, y_ref, s_ref, later_ref,
    dx_ref, dbc_ref, ddt_ref, dld_ref, carry, dgram,
):
    @pl.when(pl.program_id(0) == 0)
    def _():
        carry[...] = later_ref[...]

    cum = cum_ref[...]
    final = cum[SPAN - 1 : SPAN]
    b_low = split(bc_ref[:, :STATE])
    c_low = split(bc_ref[:, STATE:])
    gram = dot3(b_low, c_low, NT)
    later = carry[...]
    later_low = split(later)
    state = s_ref[0]
    from_state = dot3(b_low, later_low, NT)
    anti = triangle(False)
    lane = lax.broadcasted_iota(jnp.int32, (SPAN, 2 * HEADDIM), 1)
    head_lane = lax.broadcasted_iota(jnp.int32, (SPAN, heads), 1)
    row = lax.broadcasted_iota(jnp.int32, (SPAN, heads), 0)
    one_lane = lax.broadcasted_iota(jnp.int32, (1, heads), 1)
    to_end = jnp.exp(final - cum)
    grown = jnp.exp(cum)
    end_factor = jnp.exp(final)
    ddt = jnp.zeros((SPAN, heads), jnp.float32)
    dcum = jnp.zeros((SPAN, heads), jnp.float32)
    dfinal = jnp.zeros((1, heads), jnp.float32)
    dgram[...] = jnp.zeros_like(dgram)
    weighted, lifted = [], []
    for j in range(heads // 2):
        at = slice(2 * HEADDIM * j, 2 * HEADDIM * (j + 1))
        x, dy = x_ref[:, at], dy_ref[:, at]
        dt = spread(dt_ref[...], j, 2 * HEADDIM)
        xs = x * dt
        xs_low, dy_low = split(xs), split(dy)
        parts = []
        for i in range(2):
            h = 2 * j + i
            mine = (lane < HEADDIM) if i == 0 else (lane >= HEADDIM)
            gap = cumt_ref[h : h + 1, :] - cum[:, h : h + 1]
            decay = jnp.exp(jnp.where(anti, gap, -1e30))
            parts.append(dot3(split(decay * gram), dy_low, NN))
            own = split(jnp.where(mine, xs, 0.0))
            dgram[...] += decay * dot3(own, dy_low, NT)
        ends = spread(to_end, j, 2 * HEADDIM)
        state_part = ends * from_state[:, at]
        dxs = jnp.where(lane < HEADDIM, parts[0], parts[1]) + state_part
        dx_ref[:, at] = dt * dxs
        weighted.append(xs * ends)
        lifted.append(dy * spread(grown, j, 2 * HEADDIM))
        over_dt = x * dxs
        over_cum = dy * y_ref[:, at] - xs * dxs
        over_end = xs * state_part
        for i in range(2):
            h = 2 * j + i
            mine = (lane < HEADDIM) if i == 0 else (lane >= HEADDIM)
            ddt = jnp.where(
                head_lane == h, jnp.sum(jnp.where(mine, over_dt, 0.0), axis=1, keepdims=True), ddt
            )
            dcum = jnp.where(
                head_lane == h, jnp.sum(jnp.where(mine, over_cum, 0.0), axis=1, keepdims=True), dcum
            )
            ending = jnp.sum(jnp.where(mine, over_end, 0.0), axis=0, keepdims=True)
            rows = slice(h * HEADDIM, (h + 1) * HEADDIM)
            held = jnp.sum(state[rows] * later[rows], axis=0, keepdims=True)
            total = jnp.sum(ending + end_factor[:, h : h + 1] * held, axis=1, keepdims=True)
            dfinal = jnp.where(one_lane == h, total, dfinal)
    ddt_ref[...] = ddt
    dcum = jnp.where(row == SPAN - 1, dcum + dfinal, dcum)
    dld_ref[...] = ones_dot(anti.astype(jnp.bfloat16), dcum)
    weighted_low = split(jnp.concatenate(weighted, axis=1))
    lifted_low = split(jnp.concatenate(lifted, axis=1))
    dgram_low = split(dgram[...])
    dbc_ref[:, :STATE] = dot3(dgram_low, c_low, NN) + dot3(weighted_low, later_low, NN)
    dbc_ref[:, STATE:] = dot3(dgram_low, b_low, TN) + dot3(lifted_low, split(state), NN)
    carry[...] = decay_state(later, end_factor, heads) + dot3(lifted_low, c_low, TN)


def chunk_call(kernel, heads, amount, in_kinds, out_kinds, backward=False, scratch=()):
    blocks = amount // SPAN

    def at(step):
        return blocks - 1 - step if backward else step

    width = heads * HEADDIM
    kinds = {
        "wide": ((amount, width), pl.BlockSpec((SPAN, width), lambda i: (at(i), 0))),
        "head": ((amount, heads), pl.BlockSpec((SPAN, heads), lambda i: (at(i), 0))),
        "headt": ((heads, amount), pl.BlockSpec((heads, SPAN), lambda i: (0, at(i)))),
        "bc": ((amount, 2 * STATE), pl.BlockSpec((SPAN, 2 * STATE), lambda i: (at(i), 0))),
        "state": ((width, STATE), pl.BlockSpec((width, STATE), lambda i: (0, 0))),
        "states": (
            (blocks, width, STATE),
            pl.BlockSpec((1, width, STATE), lambda i: (at(i), 0, 0)),
        ),
    }
    return pl.pallas_call(
        functools.partial(kernel, heads),
        grid=(blocks,),
        in_specs=[kinds[kind][1] for kind in in_kinds],
        out_specs=[kinds[kind][1] for kind in out_kinds],
        out_shape=[jax.ShapeDtypeStruct(kinds[kind][0], jnp.float32) for kind in out_kinds],
        scratch_shapes=[pltpu.VMEM(shape, jnp.float32) for shape in scratch],
        compiler_params=pltpu.CompilerParams(
            dimension_semantics=("arbitrary",), vmem_limit_bytes=48 * 2**20
        ),
    )


def ingredients(
    value_pre, state_pre, step_pre, rim_rows,
    value_kernel, value_bias, state_kernel, state_bias, step_bias, decay_log,
):
    value_width = value_pre.shape[1]
    x_conv = conv_silu(value_pre, value_kernel, value_bias, rim_rows[:, :value_width])
    bc_conv = conv_silu(state_pre, state_kernel, state_bias, rim_rows[:, value_width:])
    step_size = jax.nn.softplus(step_pre + step_bias)
    log_decay = -step_size * jnp.exp(decay_log)
    return x_conv, bc_conv, step_size, log_decay


def chain(decays, states, backward):
    count, mine = lax.axis_size("row"), lax.axis_index("row")
    order = range(count - 1, 0, -1) if backward else range(count - 1)
    total = jnp.zeros_like(states[0])
    for position in order:
        longer = jnp.repeat(decays[position], HEADDIM)[:, None] * total + states[position]
        keep = position > mine if backward else position < mine
        total = jnp.where(keep, longer, total)
    return total


def right_product(grad_low, full_weight):
    return lax.dot_general(grad_low, full_weight, NT, preferred_element_type=jnp.float32)


def left_product(normed, grad_low):
    return lax.dot_general(normed, grad_low, TN, preferred_element_type=jnp.float32)


def col_sum(part):
    return part + lax.ppermute(part, "col", [(0, 1), (1, 0)])


def body(
    layer_input,
    norm_gain,
    gate_weight,
    value_weight,
    state_weight,
    step_weight,
    value_kernel,
    value_bias,
    state_kernel,
    state_bias,
    step_bias,
    decay_log,
    skip_gain,
    gate_gain,
    out_weight,
    out_grad,
):
    value_width, state_width = value_weight.shape[1], state_weight.shape[1]
    head_part = step_weight.shape[1]
    scan_weights = lax.all_gather(
        jnp.concatenate([value_weight, state_weight, step_weight], axis=1), "row", axis=0, tiled=True
    )
    edge_weights = lax.all_gather(
        jnp.concatenate([gate_weight, out_weight], axis=1), "row", axis=0, tiled=True
    )
    gate_full, out_full = edge_weights[:, :value_width], edge_weights[:, value_width:]
    source = layer_input.astype(jnp.float32)
    scale_in = rms_scale(source)
    normed = (source * scale_in * norm_gain).astype(jnp.bfloat16)
    scan_pre = jnp.dot(normed, scan_weights, preferred_element_type=jnp.float32)
    wide = value_width + state_width
    value_pre, state_pre, step_pre = (
        scan_pre[:, :value_width], scan_pre[:, value_width:wide], scan_pre[:, wide:],
    )
    amount = normed.shape[0]
    margin = CONV - 1
    keep_prev = jnp.where(lax.axis_index("row") == 0, 0.0, 1.0).astype(jnp.float32)
    rim_rows = from_behind(scan_pre[amount - margin :, :wide], "row", 1) * keep_prev
    (x_conv, bc_conv, step_size, log_decay), ingredients_back = jax.vjp(
        ingredients, value_pre, state_pre, step_pre, rim_rows,
        value_kernel, value_bias, state_kernel, state_bias, step_bias, decay_log,
    )
    state_shape = (value_width, STATE)
    cumulative, end_state = chunk_call(
        end_state_kernel, head_part, amount, ("wide", "head", "head", "bc"), ("head", "state")
    )(x_conv, step_size, log_decay, bc_conv)
    decay_dev = jnp.exp(jnp.sum(log_decay, axis=0))
    decays = lax.all_gather(decay_dev, "row")
    end_states = lax.all_gather(end_state, "row")
    gate_pre = jnp.dot(normed, gate_full, preferred_element_type=jnp.float32)
    cumulative_t = cumulative.T
    entry = chain(decays, end_states, False)
    y_scan, states = chunk_call(
        forward_kernel, head_part, amount,
        ("wide", "head", "head", "headt", "bc", "state"), ("wide", "states"),
        scratch=(state_shape,),
    )(x_conv, step_size, cumulative, cumulative_t, bc_conv, entry)
    skip = jnp.repeat(skip_gain, HEADDIM)
    y_flat = y_scan + skip * x_conv
    grad_mixed = jnp.dot(out_grad, out_full, preferred_element_type=jnp.float32)
    sigmoid_gate = jax.nn.sigmoid(gate_pre)
    gate_act = gate_pre * sigmoid_gate
    gated = y_flat * gate_act
    gained = grad_mixed * gate_gain
    sums = col_sum(
        jnp.stack([jnp.sum(gated * gated, axis=1), jnp.sum(gained * gated, axis=1)])
    )
    gate_scale = lax.rsqrt(sums[0] / INNER + EPSILON)[:, None]
    gate_inner = sums[1][:, None] / INNER
    grad_gated = gate_scale * gained - gated * gate_scale**3 * gate_inner
    grad_y = grad_gated * gate_act
    (grad_entry,) = chunk_call(
        entry_grad_kernel, head_part, amount, ("wide", "head", "bc"), ("state",), backward=True
    )(grad_y, cumulative, bc_conv)
    grad_entries = lax.all_gather(grad_entry, "row")
    mixed_low = (gated * gate_scale * gate_gain).astype(jnp.bfloat16)
    partial_out = right_product(mixed_low, out_full)
    summed_out = col_sum(partial_out)
    mixed_out = (source + summed_out).astype(jnp.bfloat16)
    grad_gate_pre = grad_gated * y_flat * sigmoid_gate * (1.0 + gate_pre * (1.0 - sigmoid_gate))
    gate_low = grad_gate_pre.astype(jnp.bfloat16)
    early_part = jnp.concatenate(
        [left_product(out_grad, mixed_low), left_product(normed, gate_low)], axis=1
    )
    early = lax.psum(
        lax.psum_scatter(early_part, "row", scatter_dimension=0, tiled=True), "dp"
    )
    gate_gain_part = jnp.sum(grad_mixed * gated * gate_scale, axis=0)
    skip_part = jnp.sum((x_conv * grad_y).reshape(amount, head_part, HEADDIM), axis=(0, 2))
    later_grad = chain(decays, grad_entries, True)
    grad_x, grad_bc, grad_step_size, grad_log_decay = chunk_call(
        backward_kernel, head_part, amount,
        ("wide", "head", "head", "headt", "bc", "wide", "wide", "states", "state"),
        ("wide", "bc", "head", "head"),
        backward=True, scratch=(state_shape, (SPAN, SPAN)),
    )(x_conv, step_size, cumulative, cumulative_t, bc_conv, grad_y, y_scan, states, later_grad)
    (
        grad_value_pre, grad_state_pre, grad_step_pre, grad_rim,
        grad_value_kernel, grad_value_bias, grad_state_kernel, grad_state_bias,
        grad_step_bias, grad_decay_log,
    ) = ingredients_back((grad_x + skip * grad_y, grad_bc, grad_step_size, grad_log_decay))
    from_next = from_behind(grad_rim * keep_prev, "row", -1)
    grad_scan_pre = jnp.concatenate([grad_value_pre, grad_state_pre, grad_step_pre], axis=1)
    from_next = jnp.pad(from_next, ((amount - margin, 0), (0, head_part)))
    scan_low = (grad_scan_pre + from_next).astype(jnp.bfloat16)
    grad_normed_part = right_product(gate_low, gate_full) + right_product(scan_low, scan_weights)
    grad_normed = col_sum(grad_normed_part)
    late = lax.psum_scatter(
        left_product(normed, scan_low), "row", scatter_dimension=0, tiled=True
    )
    late_state = lax.psum(late[:, value_width:wide], ("dp", "col"))
    late = lax.psum(jnp.concatenate([late[:, :value_width], late[:, wide:]], axis=1), "dp")
    gained_in = grad_normed * norm_gain
    input_inner = jnp.sum(gained_in * source, axis=1, keepdims=True)
    input_grad = (
        out_grad.astype(jnp.float32)
        + scale_in * gained_in
        - source * scale_in**3 * (input_inner / D)
    )
    norm_gain_part = jnp.sum(grad_normed_part * source * scale_in, axis=0)
    shared = (norm_gain_part, grad_state_kernel, grad_state_bias)
    own = (
        grad_value_kernel, grad_value_bias, grad_step_bias, grad_decay_log, skip_part,
        gate_gain_part,
    )
    own_flat = jnp.concatenate([part.reshape(-1) for part in own])
    col = lax.axis_index("col")
    own_slots = [jnp.where(col == i, own_flat, 0.0) for i in range(lax.axis_size("col"))]
    flat = lax.psum(
        jnp.concatenate([part.reshape(-1) for part in shared] + own_slots), ("dp", "row", "col")
    )

    def take(flat, parts):
        out, start = [], 0
        for part in parts:
            out.append(flat[start : start + part.size].reshape(part.shape))
            start += part.size
        return out

    shared_size = sum(part.size for part in shared)
    norm_gain_grad, grad_state_kernel, grad_state_bias = take(flat[:shared_size], shared)
    (
        grad_value_kernel, grad_value_bias, grad_step_bias, grad_decay_log, grad_skip_gain,
        gate_gain_grad,
    ) = take(
        lax.dynamic_slice_in_dim(flat, shared_size + col * own_flat.size, own_flat.size), own
    )
    return (
        mixed_out,
        input_grad,
        norm_gain_grad,
        early[:, value_width:],
        late[:, :value_width],
        late_state,
        late[:, value_width:],
        grad_value_kernel,
        grad_value_bias,
        grad_state_kernel,
        grad_state_bias,
        grad_step_bias,
        grad_decay_log,
        grad_skip_gain,
        gate_gain_grad,
        early[:, :value_width],
    )


def solution(mesh):
    in_specs = (
        P(("dp", "row"), None),
        P(),
        P("row", "col"),
        P("row", "col"),
        P("row", None),
        P("row", "col"),
        P(None, "col"),
        P("col"),
        P(),
        P(),
        P("col"),
        P("col"),
        P("col"),
        P("col"),
        P("row", "col"),
        P(("dp", "row"), None),
    )
    out_specs = (
        P(("dp", "row"), None),
        P(("dp", "row"), None),
        P(),
        P("row", "col"),
        P("row", "col"),
        P("row", None),
        P("row", "col"),
        P(None, "col"),
        P("col"),
        P(),
        P(),
        P("col"),
        P("col"),
        P("col"),
        P("col"),
        P("row", "col"),
    )
    return jax.shard_map(body, mesh=mesh, in_specs=in_specs, out_specs=out_specs, check_vma=False)
```

```python
import functools

import jax
import jax.numpy as jnp
from jax import lax
from jax.experimental import pallas as pl
from jax.experimental.pallas import tpu as pltpu
from jax.sharding import PartitionSpec as P

D = 768
HEADDIM = 64
STATE = 128
CONV = 4
SPAN = 256
INNER = 1536


EPSILON = 1e-05
HIGHEST = lax.Precision.HIGHEST


def from_behind(x, axis, by):
    peers = lax.axis_size(axis)
    pairs = [(i, i + by) for i in range(peers) if 0 <= i + by < peers]
    return lax.ppermute(x, axis, pairs)


def entering(value, axis, join, neutral, backward):
    count, mine = (lax.axis_size(axis), lax.axis_index(axis))
    pieces = jax.tree.map(lambda part: lax.all_gather(part, axis), value)
    if backward:
        pieces = jax.tree.map(lambda part: part[::-1], pieces)
        mine = count - 1 - mine
    total = jax.tree.map(
        lambda part, zero: jnp.full_like(part, 0) + jnp.asarray(zero, part.dtype), value, neutral
    )

    def turn(position, total):
        longer = join(total, jax.tree.map(lambda part: part[position], pieces))
        return jax.tree.map(lambda new, old: jnp.where(position < mine, new, old), longer, total)

    return lax.fori_loop(0, count - 1, turn, total)


def rms_scale(values):
    return lax.rsqrt(jnp.mean(values * values, axis=-1, keepdims=True) + EPSILON)


def conv_silu(before, kernel, kernel_bias, margin_rows):
    extended = jnp.concatenate([margin_rows, before], axis=0)
    amount = before.shape[0]
    tap_count = kernel.shape[0]
    summed = kernel_bias[None, :] + sum(
        (
            kernel[tap_index][None, :] * extended[tap_index : tap_index + amount]
            for tap_index in range(tap_count)
        )
    )
    return jax.nn.silu(summed)


NN = (((1,), (0,)), ((), ()))
NT = (((1,), (1,)), ((), ()))
TN = (((0,), (0,)), ((), ()))


def split(v):
    high = v.astype(jnp.bfloat16)
    return high, (v - high.astype(jnp.float32)).astype(jnp.bfloat16)


def dot3(a, b, dims):
    def product(u, v):
        return lax.dot_general(u, v, dims, preferred_element_type=jnp.float32)

    return product(a[0], b[0]) + (product(a[0], b[1]) + product(a[1], b[0]))


def ones_dot(ones, v):
    first, second = split(v)
    third = (v - first.astype(jnp.float32) - second.astype(jnp.float32)).astype(jnp.bfloat16)

    def product(u):
        return lax.dot_general(ones, u, NN, preferred_element_type=jnp.float32)

    return product(first) + (product(second) + product(third))


def spread(per_head, pair, width):
    rows = per_head.shape[0]
    lane = lax.broadcasted_iota(jnp.int32, (rows, width), 1)
    low = jnp.broadcast_to(per_head[:, 2 * pair : 2 * pair + 1], (rows, width))
    high = jnp.broadcast_to(per_head[:, 2 * pair + 1 : 2 * pair + 2], (rows, width))
    return jnp.where(lane < HEADDIM, low, high)


def spread_all(per_head, heads):
    return jnp.concatenate([spread(per_head, j, 2 * HEADDIM) for j in range(heads // 2)], axis=1)


def decay_state(state, factor, heads):
    return jnp.concatenate(
        [state[h * HEADDIM : (h + 1) * HEADDIM] * factor[:, h : h + 1] for h in range(heads)],
        axis=0,
    )


def triangle(lower):
    rows = lax.broadcasted_iota(jnp.int32, (SPAN, SPAN), 0)
    cols = lax.broadcasted_iota(jnp.int32, (SPAN, SPAN), 1)
    return rows >= cols if lower else rows <= cols


def end_state_kernel(heads, x_ref, dt_ref, ld_ref, bc_ref, cum_ref, end_ref):
    @pl.when(pl.program_id(0) == 0)
    def _():
        end_ref[...] = jnp.zeros_like(end_ref)

    ones = triangle(True).astype(jnp.bfloat16)
    cum = ones_dot(ones, ld_ref[...])
    cum_ref[...] = cum
    final = cum[SPAN - 1 : SPAN]
    weighted = x_ref[...] * spread_all(dt_ref[...] * jnp.exp(final - cum), heads)
    added = dot3(split(weighted), split(bc_ref[:, :STATE]), TN)
    end_ref[...] = decay_state(end_ref[...], jnp.exp(final), heads) + added


def forward_kernel(heads, x_ref, dt_ref, cum_ref, cumt_ref, bc_ref, entry_ref, y_ref, s_ref, state):
    @pl.when(pl.program_id(0) == 0)
    def _():
        state[...] = entry_ref[...]

    cum = cum_ref[...]
    final = cum[SPAN - 1 : SPAN]
    b_low = split(bc_ref[:, :STATE])
    c_low = split(bc_ref[:, STATE:])
    gram = dot3(c_low, b_low, NT)
    carry = state[...]
    s_ref[0] = carry
    carried = dot3(c_low, split(carry), NT)
    causal = triangle(True)
    lane = lax.broadcasted_iota(jnp.int32, (SPAN, 2 * HEADDIM), 1)
    to_end = jnp.exp(final - cum)
    grown = jnp.exp(cum)
    weighted = []
    for j in range(heads // 2):
        at = slice(2 * HEADDIM * j, 2 * HEADDIM * (j + 1))
        xs = x_ref[:, at] * spread(dt_ref[...], j, 2 * HEADDIM)
        xs_low = split(xs)
        parts = []
        for h in (2 * j, 2 * j + 1):
            gap = cum[:, h : h + 1] - cumt_ref[h : h + 1, :]
            decay = jnp.exp(jnp.where(causal, gap, -1e30))
            parts.append(dot3(split(decay * gram), xs_low, NN))
        within = jnp.where(lane < HEADDIM, parts[0], parts[1])
        y_ref[:, at] = within + spread(grown, j, 2 * HEADDIM) * carried[:, at]
        weighted.append(xs * spread(to_end, j, 2 * HEADDIM))
    added = dot3(split(jnp.concatenate(weighted, axis=1)), b_low, TN)
    state[...] = decay_state(carry, jnp.exp(final), heads) + added


def entry_grad_kernel(heads, dy_ref, cum_ref, bc_ref, out_ref):
    @pl.when(pl.program_id(0) == 0)
    def _():
        out_ref[...] = jnp.zeros_like(out_ref)

    cum = cum_ref[...]
    grown = dy_ref[...] * spread_all(jnp.exp(cum), heads)
    added = dot3(split(grown), split(bc_ref[:, STATE:]), TN)
    out_ref[...] = decay_state(out_ref[...], jnp.exp(cum[SPAN - 1 : SPAN]), heads) + added


def backward_kernel(
    heads, x_ref, dt_ref, cum_ref, cumt_ref, bc_ref, dy_ref, y_ref, s_ref, later_ref,
    dx_ref, dbc_ref, ddt_ref, dld_ref, carry, dgram,
):
    @pl.when(pl.program_id(0) == 0)
    def _():
        carry[...] = later_ref[...]

    cum = cum_ref[...]
    final = cum[SPAN - 1 : SPAN]
    b_low = split(bc_ref[:, :STATE])
    c_low = split(bc_ref[:, STATE:])
    gram = dot3(b_low, c_low, NT)
    later = carry[...]
    later_low = split(later)
    state = s_ref[0]
    from_state = dot3(b_low, later_low, NT)
    anti = triangle(False)
    lane = lax.broadcasted_iota(jnp.int32, (SPAN, 2 * HEADDIM), 1)
    head_lane = lax.broadcasted_iota(jnp.int32, (SPAN, heads), 1)
    row = lax.broadcasted_iota(jnp.int32, (SPAN, heads), 0)
    one_lane = lax.broadcasted_iota(jnp.int32, (1, heads), 1)
    to_end = jnp.exp(final - cum)
    grown = jnp.exp(cum)
    end_factor = jnp.exp(final)
    ddt = jnp.zeros((SPAN, heads), jnp.float32)
    dcum = jnp.zeros((SPAN, heads), jnp.float32)
    dfinal = jnp.zeros((1, heads), jnp.float32)
    dgram[...] = jnp.zeros_like(dgram)
    weighted, lifted = [], []
    for j in range(heads // 2):
        at = slice(2 * HEADDIM * j, 2 * HEADDIM * (j + 1))
        x, dy = x_ref[:, at], dy_ref[:, at]
        dt = spread(dt_ref[...], j, 2 * HEADDIM)
        xs = x * dt
        xs_low, dy_low = split(xs), split(dy)
        parts = []
        for i in range(2):
            h = 2 * j + i
            mine = (lane < HEADDIM) if i == 0 else (lane >= HEADDIM)
            gap = cumt_ref[h : h + 1, :] - cum[:, h : h + 1]
            decay = jnp.exp(jnp.where(anti, gap, -1e30))
            parts.append(dot3(split(decay * gram), dy_low, NN))
            own = split(jnp.where(mine, xs, 0.0))
            dgram[...] += decay * dot3(own, dy_low, NT)
        ends = spread(to_end, j, 2 * HEADDIM)
        state_part = ends * from_state[:, at]
        dxs = jnp.where(lane < HEADDIM, parts[0], parts[1]) + state_part
        dx_ref[:, at] = dt * dxs
        weighted.append(xs * ends)
        lifted.append(dy * spread(grown, j, 2 * HEADDIM))
        over_dt = x * dxs
        over_cum = dy * y_ref[:, at] - xs * dxs
        over_end = xs * state_part
        for i in range(2):
            h = 2 * j + i
            mine = (lane < HEADDIM) if i == 0 else (lane >= HEADDIM)
            ddt = jnp.where(
                head_lane == h, jnp.sum(jnp.where(mine, over_dt, 0.0), axis=1, keepdims=True), ddt
            )
            dcum = jnp.where(
                head_lane == h, jnp.sum(jnp.where(mine, over_cum, 0.0), axis=1, keepdims=True), dcum
            )
            ending = jnp.sum(jnp.where(mine, over_end, 0.0), axis=0, keepdims=True)
            rows = slice(h * HEADDIM, (h + 1) * HEADDIM)
            held = jnp.sum(state[rows] * later[rows], axis=0, keepdims=True)
            total = jnp.sum(ending + end_factor[:, h : h + 1] * held, axis=1, keepdims=True)
            dfinal = jnp.where(one_lane == h, total, dfinal)
    ddt_ref[...] = ddt
    dcum = jnp.where(row == SPAN - 1, dcum + dfinal, dcum)
    dld_ref[...] = ones_dot(anti.astype(jnp.bfloat16), dcum)
    weighted_low = split(jnp.concatenate(weighted, axis=1))
    lifted_low = split(jnp.concatenate(lifted, axis=1))
    dgram_low = split(dgram[...])
    dbc_ref[:, :STATE] = dot3(dgram_low, c_low, NN) + dot3(weighted_low, later_low, NN)
    dbc_ref[:, STATE:] = dot3(dgram_low, b_low, TN) + dot3(lifted_low, split(state), NN)
    carry[...] = decay_state(later, end_factor, heads) + dot3(lifted_low, c_low, TN)


def chunk_call(
    kernel, heads, amount, in_kinds, out_kinds, backward=False, scratch=(), flops=4096
):
    blocks = amount // SPAN

    def at(step):
        return blocks - 1 - step if backward else step

    width = heads * HEADDIM
    kinds = {
        "wide": ((amount, width), pl.BlockSpec((SPAN, width), lambda i: (at(i), 0))),
        "head": ((amount, heads), pl.BlockSpec((SPAN, heads), lambda i: (at(i), 0))),
        "headt": ((heads, amount), pl.BlockSpec((heads, SPAN), lambda i: (0, at(i)))),
        "bc": ((amount, 2 * STATE), pl.BlockSpec((SPAN, 2 * STATE), lambda i: (at(i), 0))),
        "state": ((width, STATE), pl.BlockSpec((width, STATE), lambda i: (0, 0))),
        "states": (
            (blocks, width, STATE),
            pl.BlockSpec((1, width, STATE), lambda i: (at(i), 0, 0)),
        ),
    }
    return pl.pallas_call(
        functools.partial(kernel, heads),
        grid=(blocks,),
        in_specs=[kinds[kind][1] for kind in in_kinds],
        out_specs=[kinds[kind][1] for kind in out_kinds],
        out_shape=[jax.ShapeDtypeStruct(kinds[kind][0], jnp.float32) for kind in out_kinds],
        scratch_shapes=[pltpu.VMEM(shape, jnp.float32) for shape in scratch],
        cost_estimate=pl.CostEstimate(
            flops=flops * amount * width, bytes_accessed=2**24, transcendentals=amount * width
        ),
        compiler_params=pltpu.CompilerParams(
            dimension_semantics=("arbitrary",), vmem_limit_bytes=48 * 2**20
        ),
    )


def ingredients(
    value_pre, state_pre, step_pre, rim_rows,
    value_kernel, value_bias, state_kernel, state_bias, step_bias, decay_log,
):
    value_width = value_pre.shape[1]
    x_conv = conv_silu(value_pre, value_kernel, value_bias, rim_rows[:, :value_width])
    bc_conv = conv_silu(state_pre, state_kernel, state_bias, rim_rows[:, value_width:])
    step_size = jax.nn.softplus(step_pre + step_bias)
    log_decay = -step_size * jnp.exp(decay_log)
    return x_conv, bc_conv, step_size, log_decay


def chain(decay, states, way):
    factor = jnp.ones_like(decay)
    total = from_behind(states, "row", way)
    for by in range(1, lax.axis_size("row") - 1):
        factor = factor * from_behind(decay, "row", way * by)
        piece = from_behind(states, "row", way * (by + 1))
        total = total + jnp.repeat(factor, HEADDIM)[:, None] * piece
    return total


def butterfly(part, axis):
    peers = lax.axis_size(axis)
    by = 1
    while by < peers:
        part = part + lax.ppermute(part, axis, [(i, i ^ by) for i in range(peers)])
        by *= 2
    return part


def halves_in(part, axis):
    peers, me = lax.axis_size(axis), lax.axis_index(axis)
    by = 1
    while by < peers:
        odd = (me // by) % 2 == 1
        half = part.shape[0] // 2
        first, second = part[:half], part[half:]
        given = lax.ppermute(
            jnp.where(odd, first, second), axis, [(i, i ^ by) for i in range(peers)]
        )
        part = jnp.where(odd, second, first) + given
        by *= 2
    return part


def halves_out(part, axis):
    peers, me = lax.axis_size(axis), lax.axis_index(axis)
    by = peers // 2
    while by >= 1:
        odd = (me // by) % 2 == 1
        given = lax.ppermute(part, axis, [(i, i ^ by) for i in range(peers)])
        part = jnp.concatenate([jnp.where(odd, given, part), jnp.where(odd, part, given)], axis=0)
        by //= 2
    return part


def right_product(grad_low, full_weight):
    return lax.dot_general(grad_low, full_weight, NT, preferred_element_type=jnp.float32)


def left_product(normed, grad_low):
    return lax.dot_general(normed, grad_low, TN, preferred_element_type=jnp.float32)


def col_sum(part):
    return part + lax.ppermute(part, "col", [(0, 1), (1, 0)])


def body(
    layer_input,
    norm_gain,
    gate_weight,
    value_weight,
    state_weight,
    step_weight,
    value_kernel,
    value_bias,
    state_kernel,
    state_bias,
    step_bias,
    decay_log,
    skip_gain,
    gate_gain,
    out_weight,
    out_grad,
):
    value_width, state_width = value_weight.shape[1], state_weight.shape[1]
    head_part = step_weight.shape[1]
    scan_weights = lax.all_gather(
        jnp.concatenate([value_weight, state_weight, step_weight], axis=1), "row", axis=0, tiled=True
    )
    edge_weights = lax.all_gather(
        jnp.concatenate([gate_weight, out_weight], axis=1), "row", axis=0, tiled=True
    )
    gate_full, out_full = edge_weights[:, :value_width], edge_weights[:, value_width:]
    source = layer_input.astype(jnp.float32)
    scale_in = rms_scale(source)
    normed = (source * scale_in * norm_gain).astype(jnp.bfloat16)
    scan_pre = jnp.dot(normed, scan_weights, preferred_element_type=jnp.float32)
    wide = value_width + state_width
    value_pre, state_pre, step_pre = (
        scan_pre[:, :value_width], scan_pre[:, value_width:wide], scan_pre[:, wide:],
    )
    amount = normed.shape[0]
    margin = CONV - 1
    keep_prev = jnp.where(lax.axis_index("row") == 0, 0.0, 1.0).astype(jnp.float32)
    rim_rows = from_behind(scan_pre[amount - margin :, :wide], "row", 1) * keep_prev
    (x_conv, bc_conv, step_size, log_decay), ingredients_back = jax.vjp(
        ingredients, value_pre, state_pre, step_pre, rim_rows,
        value_kernel, value_bias, state_kernel, state_bias, step_bias, decay_log,
    )
    state_shape = (value_width, STATE)
    cumulative, end_state = chunk_call(
        end_state_kernel, head_part, amount, ("wide", "head", "head", "bc"), ("head", "state")
    )(x_conv, step_size, log_decay, bc_conv)
    decay_dev = jnp.exp(jnp.sum(log_decay, axis=0))
    gate_pre = jnp.dot(normed, gate_full, preferred_element_type=jnp.float32)
    cumulative_t = cumulative.T
    entry = chain(decay_dev, end_state, 1)
    y_scan, states = chunk_call(
        forward_kernel, head_part, amount,
        ("wide", "head", "head", "headt", "bc", "state"), ("wide", "states"),
        scratch=(state_shape,),
    )(x_conv, step_size, cumulative, cumulative_t, bc_conv, entry)
    skip = jnp.repeat(skip_gain, HEADDIM)
    y_flat = y_scan + skip * x_conv
    grad_mixed = jnp.dot(out_grad, out_full, preferred_element_type=jnp.float32)
    sigmoid_gate = jax.nn.sigmoid(gate_pre)
    gate_act = gate_pre * sigmoid_gate
    gated = y_flat * gate_act
    gained = grad_mixed * gate_gain
    sums = col_sum(
        jnp.stack([jnp.sum(gated * gated, axis=1), jnp.sum(gained * gated, axis=1)])
    )
    gate_scale = lax.rsqrt(sums[0] / INNER + EPSILON)[:, None]
    gate_inner = sums[1][:, None] / INNER
    grad_gated = gate_scale * gained - gated * gate_scale**3 * gate_inner
    grad_y = grad_gated * gate_act
    (grad_entry,) = chunk_call(
        entry_grad_kernel, head_part, amount, ("wide", "head", "bc"), ("state",), backward=True
    )(grad_y, cumulative, bc_conv)
    mixed_low = (gated * gate_scale * gate_gain).astype(jnp.bfloat16)
    partial_out = right_product(mixed_low, out_full)
    summed_out = col_sum(partial_out)
    grad_gate_pre = grad_gated * y_flat * sigmoid_gate * (1.0 + gate_pre * (1.0 - sigmoid_gate))
    gate_low = grad_gate_pre.astype(jnp.bfloat16)
    early_part = jnp.concatenate(
        [left_product(out_grad, mixed_low), left_product(normed, gate_low)], axis=1
    )
    gate_gain_part = jnp.sum(grad_mixed * gated * gate_scale, axis=0)
    skip_part = jnp.sum((x_conv * grad_y).reshape(amount, head_part, HEADDIM), axis=(0, 2))
    later_grad = chain(decay_dev, grad_entry, -1)
    early_part, later_grad = lax.optimization_barrier((early_part, later_grad))
    early = lax.psum_scatter(early_part, "row", scatter_dimension=0, tiled=True)
    grad_x, grad_bc, grad_step_size, grad_log_decay = chunk_call(
        backward_kernel, head_part, amount,
        ("wide", "head", "head", "headt", "bc", "wide", "wide", "states", "state"),
        ("wide", "bc", "head", "head"),
        backward=True, scratch=(state_shape, (SPAN, SPAN)), flops=16384,
    )(x_conv, step_size, cumulative, cumulative_t, bc_conv, grad_y, y_scan, states, later_grad)
    grad_x, summed_out = lax.optimization_barrier((grad_x, summed_out))
    mixed_out = (source + summed_out).astype(jnp.bfloat16)
    (
        grad_value_pre, grad_state_pre, grad_step_pre, grad_rim,
        grad_value_kernel, grad_value_bias, grad_state_kernel, grad_state_bias,
        grad_step_bias, grad_decay_log,
    ) = ingredients_back((grad_x + skip * grad_y, grad_bc, grad_step_size, grad_log_decay))
    from_next = from_behind(grad_rim * keep_prev, "row", -1)
    grad_scan_pre = jnp.concatenate([grad_value_pre, grad_state_pre, grad_step_pre], axis=1)
    from_next = jnp.pad(from_next, ((amount - margin, 0), (0, head_part)))
    scan_low = (grad_scan_pre + from_next).astype(jnp.bfloat16)
    scan_low, early = lax.optimization_barrier((scan_low, early))
    early = halves_in(early, "dp")
    grad_normed_part = right_product(gate_low, gate_full) + right_product(scan_low, scan_weights)
    grad_normed = col_sum(grad_normed_part)
    late = lax.psum_scatter(
        left_product(normed, scan_low), "row", scatter_dimension=0, tiled=True
    )
    late = jnp.concatenate(
        [late[:, :value_width], col_sum(late[:, value_width:wide]), late[:, wide:]], axis=1
    )
    late, early = lax.optimization_barrier((late, early))
    early = halves_out(early, "dp")
    late = halves_out(halves_in(late, "dp"), "dp")
    gained_in = grad_normed * norm_gain
    input_inner = jnp.sum(gained_in * source, axis=1, keepdims=True)
    input_grad = (
        out_grad.astype(jnp.float32)
        + scale_in * gained_in
        - source * scale_in**3 * (input_inner / D)
    )
    norm_gain_part = jnp.sum(grad_normed_part * source * scale_in, axis=0)
    shared = (norm_gain_part, grad_state_kernel, grad_state_bias)
    own = (
        grad_value_kernel, grad_value_bias, grad_step_bias, grad_decay_log, skip_part,
        gate_gain_part,
    )
    own_flat = jnp.concatenate([part.reshape(-1) for part in own])
    col = lax.axis_index("col")
    own_slots = [jnp.where(col == i, own_flat, 0.0) for i in range(lax.axis_size("col"))]
    flat = jnp.concatenate([part.reshape(-1) for part in shared] + own_slots)
    for axis in ("row", "col", "dp"):
        flat = butterfly(flat, axis)

    def take(flat, parts):
        out, start = [], 0
        for part in parts:
            out.append(flat[start : start + part.size].reshape(part.shape))
            start += part.size
        return out

    shared_size = sum(part.size for part in shared)
    norm_gain_grad, grad_state_kernel, grad_state_bias = take(flat[:shared_size], shared)
    (
        grad_value_kernel, grad_value_bias, grad_step_bias, grad_decay_log, grad_skip_gain,
        gate_gain_grad,
    ) = take(
        lax.dynamic_slice_in_dim(flat, shared_size + col * own_flat.size, own_flat.size), own
    )
    return (
        mixed_out,
        input_grad,
        norm_gain_grad,
        early[:, value_width:],
        late[:, :value_width],
        late[:, value_width:wide],
        late[:, wide:],
        grad_value_kernel,
        grad_value_bias,
        grad_state_kernel,
        grad_state_bias,
        grad_step_bias,
        grad_decay_log,
        grad_skip_gain,
        gate_gain_grad,
        early[:, :value_width],
    )


def solution(mesh):
    in_specs = (
        P(("dp", "row"), None),
        P(),
        P("row", "col"),
        P("row", "col"),
        P("row", None),
        P("row", "col"),
        P(None, "col"),
        P("col"),
        P(),
        P(),
        P("col"),
        P("col"),
        P("col"),
        P("col"),
        P("row", "col"),
        P(("dp", "row"), None),
    )
    out_specs = (
        P(("dp", "row"), None),
        P(("dp", "row"), None),
        P(),
        P("row", "col"),
        P("row", "col"),
        P("row", None),
        P("row", "col"),
        P(None, "col"),
        P("col"),
        P(),
        P(),
        P("col"),
        P("col"),
        P("col"),
        P("col"),
        P("row", "col"),
    )
    return jax.shard_map(body, mesh=mesh, in_specs=in_specs, out_specs=out_specs, check_vma=False)
```

```python
import functools

import jax
import jax.numpy as jnp
from jax import lax
from jax.experimental import pallas as pl
from jax.experimental.pallas import tpu as pltpu
from jax.sharding import PartitionSpec as P

D = 768
HEADDIM = 64
STATE = 128
CONV = 4
SPAN = 256
INNER = 1536


EPSILON = 1e-05
HIGHEST = lax.Precision.HIGHEST


def from_behind(x, axis, by):
    peers = lax.axis_size(axis)
    pairs = [(i, i + by) for i in range(peers) if 0 <= i + by < peers]
    return lax.ppermute(x, axis, pairs)


def entering(value, axis, join, neutral, backward):
    count, mine = (lax.axis_size(axis), lax.axis_index(axis))
    pieces = jax.tree.map(lambda part: lax.all_gather(part, axis), value)
    if backward:
        pieces = jax.tree.map(lambda part: part[::-1], pieces)
        mine = count - 1 - mine
    total = jax.tree.map(
        lambda part, zero: jnp.full_like(part, 0) + jnp.asarray(zero, part.dtype), value, neutral
    )

    def turn(position, total):
        longer = join(total, jax.tree.map(lambda part: part[position], pieces))
        return jax.tree.map(lambda new, old: jnp.where(position < mine, new, old), longer, total)

    return lax.fori_loop(0, count - 1, turn, total)


def rms_scale(values):
    return lax.rsqrt(jnp.mean(values * values, axis=-1, keepdims=True) + EPSILON)


def conv_silu(before, kernel, kernel_bias, margin_rows):
    extended = jnp.concatenate([margin_rows, before], axis=0)
    amount = before.shape[0]
    tap_count = kernel.shape[0]
    summed = kernel_bias[None, :] + sum(
        (
            kernel[tap_index][None, :] * extended[tap_index : tap_index + amount]
            for tap_index in range(tap_count)
        )
    )
    return jax.nn.silu(summed)


NN = (((1,), (0,)), ((), ()))
NT = (((1,), (1,)), ((), ()))
TN = (((0,), (0,)), ((), ()))


def split(v):
    high = v.astype(jnp.bfloat16)
    return high, (v - high.astype(jnp.float32)).astype(jnp.bfloat16)


def dot3(a, b, dims):
    def product(u, v):
        return lax.dot_general(u, v, dims, preferred_element_type=jnp.float32)

    return product(a[0], b[0]) + (product(a[0], b[1]) + product(a[1], b[0]))


def ones_dot(ones, v):
    first, second = split(v)
    third = (v - first.astype(jnp.float32) - second.astype(jnp.float32)).astype(jnp.bfloat16)

    def product(u):
        return lax.dot_general(ones, u, NN, preferred_element_type=jnp.float32)

    return product(first) + (product(second) + product(third))


def spread(per_head, pair, width):
    rows = per_head.shape[0]
    lane = lax.broadcasted_iota(jnp.int32, (rows, width), 1)
    low = jnp.broadcast_to(per_head[:, 2 * pair : 2 * pair + 1], (rows, width))
    high = jnp.broadcast_to(per_head[:, 2 * pair + 1 : 2 * pair + 2], (rows, width))
    return jnp.where(lane < HEADDIM, low, high)


def spread_all(per_head, heads):
    return jnp.concatenate([spread(per_head, j, 2 * HEADDIM) for j in range(heads // 2)], axis=1)


def decay_state(state, factor, heads):
    return jnp.concatenate(
        [state[h * HEADDIM : (h + 1) * HEADDIM] * factor[:, h : h + 1] for h in range(heads)],
        axis=0,
    )


def triangle(lower):
    rows = lax.broadcasted_iota(jnp.int32, (SPAN, SPAN), 0)
    cols = lax.broadcasted_iota(jnp.int32, (SPAN, SPAN), 1)
    return rows >= cols if lower else rows <= cols


def end_state_kernel(heads, x_ref, dt_ref, ld_ref, bc_ref, cum_ref, end_ref):
    @pl.when(pl.program_id(0) == 0)
    def _():
        end_ref[...] = jnp.zeros_like(end_ref)

    ones = triangle(True).astype(jnp.bfloat16)
    cum = ones_dot(ones, ld_ref[...])
    cum_ref[...] = cum
    final = cum[SPAN - 1 : SPAN]
    weighted = x_ref[...] * spread_all(dt_ref[...] * jnp.exp(final - cum), heads)
    added = dot3(split(weighted), split(bc_ref[:, :STATE]), TN)
    end_ref[...] = decay_state(end_ref[...], jnp.exp(final), heads) + added


def forward_kernel(heads, x_ref, dt_ref, cum_ref, cumt_ref, bc_ref, entry_ref, y_ref, s_ref, state):
    @pl.when(pl.program_id(0) == 0)
    def _():
        state[...] = entry_ref[...]

    cum = cum_ref[...]
    final = cum[SPAN - 1 : SPAN]
    b_low = split(bc_ref[:, :STATE])
    c_low = split(bc_ref[:, STATE:])
    gram = dot3(c_low, b_low, NT)
    carry = state[...]
    s_ref[0] = carry
    carried = dot3(c_low, split(carry), NT)
    causal = triangle(True)
    lane = lax.broadcasted_iota(jnp.int32, (SPAN, 2 * HEADDIM), 1)
    to_end = jnp.exp(final - cum)
    grown = jnp.exp(cum)
    weighted = []
    for j in range(heads // 2):
        at = slice(2 * HEADDIM * j, 2 * HEADDIM * (j + 1))
        xs = x_ref[:, at] * spread(dt_ref[...], j, 2 * HEADDIM)
        xs_low = split(xs)
        parts = []
        for h in (2 * j, 2 * j + 1):
            gap = cum[:, h : h + 1] - cumt_ref[h : h + 1, :]
            decay = jnp.exp(jnp.where(causal, gap, -1e30))
            parts.append(dot3(split(decay * gram), xs_low, NN))
        within = jnp.where(lane < HEADDIM, parts[0], parts[1])
        y_ref[:, at] = within + spread(grown, j, 2 * HEADDIM) * carried[:, at]
        weighted.append(xs * spread(to_end, j, 2 * HEADDIM))
    added = dot3(split(jnp.concatenate(weighted, axis=1)), b_low, TN)
    state[...] = decay_state(carry, jnp.exp(final), heads) + added


def entry_grad_kernel(heads, dy_ref, cum_ref, bc_ref, out_ref):
    @pl.when(pl.program_id(0) == 0)
    def _():
        out_ref[...] = jnp.zeros_like(out_ref)

    cum = cum_ref[...]
    grown = dy_ref[...] * spread_all(jnp.exp(cum), heads)
    added = dot3(split(grown), split(bc_ref[:, STATE:]), TN)
    out_ref[...] = decay_state(out_ref[...], jnp.exp(cum[SPAN - 1 : SPAN]), heads) + added


def backward_kernel(
    heads, x_ref, dt_ref, cum_ref, cumt_ref, bc_ref, dy_ref, y_ref, s_ref, later_ref,
    dx_ref, dbc_ref, ddt_ref, dld_ref, carry, dgram,
):
    @pl.when(pl.program_id(0) == 0)
    def _():
        carry[...] = later_ref[...]

    cum = cum_ref[...]
    final = cum[SPAN - 1 : SPAN]
    b_low = split(bc_ref[:, :STATE])
    c_low = split(bc_ref[:, STATE:])
    gram = dot3(b_low, c_low, NT)
    later = carry[...]
    later_low = split(later)
    state = s_ref[0]
    from_state = dot3(b_low, later_low, NT)
    anti = triangle(False)
    lane = lax.broadcasted_iota(jnp.int32, (SPAN, 2 * HEADDIM), 1)
    head_lane = lax.broadcasted_iota(jnp.int32, (SPAN, heads), 1)
    row = lax.broadcasted_iota(jnp.int32, (SPAN, heads), 0)
    one_lane = lax.broadcasted_iota(jnp.int32, (1, heads), 1)
    to_end = jnp.exp(final - cum)
    grown = jnp.exp(cum)
    end_factor = jnp.exp(final)
    ddt = jnp.zeros((SPAN, heads), jnp.float32)
    dcum = jnp.zeros((SPAN, heads), jnp.float32)
    dfinal = jnp.zeros((1, heads), jnp.float32)
    dgram[...] = jnp.zeros_like(dgram)
    weighted, lifted = [], []
    for j in range(heads // 2):
        at = slice(2 * HEADDIM * j, 2 * HEADDIM * (j + 1))
        x, dy = x_ref[:, at], dy_ref[:, at]
        dt = spread(dt_ref[...], j, 2 * HEADDIM)
        xs = x * dt
        xs_low, dy_low = split(xs), split(dy)
        parts = []
        for i in range(2):
            h = 2 * j + i
            mine = (lane < HEADDIM) if i == 0 else (lane >= HEADDIM)
            gap = cumt_ref[h : h + 1, :] - cum[:, h : h + 1]
            decay = jnp.exp(jnp.where(anti, gap, -1e30))
            parts.append(dot3(split(decay * gram), dy_low, NN))
            own = split(jnp.where(mine, xs, 0.0))
            dgram[...] += decay * dot3(own, dy_low, NT)
        ends = spread(to_end, j, 2 * HEADDIM)
        state_part = ends * from_state[:, at]
        dxs = jnp.where(lane < HEADDIM, parts[0], parts[1]) + state_part
        dx_ref[:, at] = dt * dxs
        weighted.append(xs * ends)
        lifted.append(dy * spread(grown, j, 2 * HEADDIM))
        over_dt = x * dxs
        over_cum = dy * y_ref[:, at] - xs * dxs
        over_end = xs * state_part
        for i in range(2):
            h = 2 * j + i
            mine = (lane < HEADDIM) if i == 0 else (lane >= HEADDIM)
            ddt = jnp.where(
                head_lane == h, jnp.sum(jnp.where(mine, over_dt, 0.0), axis=1, keepdims=True), ddt
            )
            dcum = jnp.where(
                head_lane == h, jnp.sum(jnp.where(mine, over_cum, 0.0), axis=1, keepdims=True), dcum
            )
            ending = jnp.sum(jnp.where(mine, over_end, 0.0), axis=0, keepdims=True)
            rows = slice(h * HEADDIM, (h + 1) * HEADDIM)
            held = jnp.sum(state[rows] * later[rows], axis=0, keepdims=True)
            total = jnp.sum(ending + end_factor[:, h : h + 1] * held, axis=1, keepdims=True)
            dfinal = jnp.where(one_lane == h, total, dfinal)
    ddt_ref[...] = ddt
    dcum = jnp.where(row == SPAN - 1, dcum + dfinal, dcum)
    dld_ref[...] = ones_dot(anti.astype(jnp.bfloat16), dcum)
    weighted_low = split(jnp.concatenate(weighted, axis=1))
    lifted_low = split(jnp.concatenate(lifted, axis=1))
    dgram_low = split(dgram[...])
    dbc_ref[:, :STATE] = dot3(dgram_low, c_low, NN) + dot3(weighted_low, later_low, NN)
    dbc_ref[:, STATE:] = dot3(dgram_low, b_low, TN) + dot3(lifted_low, split(state), NN)
    carry[...] = decay_state(later, end_factor, heads) + dot3(lifted_low, c_low, TN)


def chunk_call(
    kernel, heads, amount, in_kinds, out_kinds, backward=False, scratch=(), flops=4096
):
    blocks = amount // SPAN

    def at(step):
        return blocks - 1 - step if backward else step

    width = heads * HEADDIM
    kinds = {
        "wide": ((amount, width), pl.BlockSpec((SPAN, width), lambda i: (at(i), 0))),
        "head": ((amount, heads), pl.BlockSpec((SPAN, heads), lambda i: (at(i), 0))),
        "headt": ((heads, amount), pl.BlockSpec((heads, SPAN), lambda i: (0, at(i)))),
        "bc": ((amount, 2 * STATE), pl.BlockSpec((SPAN, 2 * STATE), lambda i: (at(i), 0))),
        "state": ((width, STATE), pl.BlockSpec((width, STATE), lambda i: (0, 0))),
        "states": (
            (blocks, width, STATE),
            pl.BlockSpec((1, width, STATE), lambda i: (at(i), 0, 0)),
        ),
    }
    return pl.pallas_call(
        functools.partial(kernel, heads),
        grid=(blocks,),
        in_specs=[kinds[kind][1] for kind in in_kinds],
        out_specs=[kinds[kind][1] for kind in out_kinds],
        out_shape=[jax.ShapeDtypeStruct(kinds[kind][0], jnp.float32) for kind in out_kinds],
        scratch_shapes=[pltpu.VMEM(shape, jnp.float32) for shape in scratch],
        cost_estimate=pl.CostEstimate(
            flops=flops * amount * width, bytes_accessed=2**24, transcendentals=amount * width
        ),
        compiler_params=pltpu.CompilerParams(
            dimension_semantics=("arbitrary",), vmem_limit_bytes=48 * 2**20
        ),
    )


def ingredients(
    value_pre, state_pre, step_pre, rim_rows,
    value_kernel, value_bias, state_kernel, state_bias, step_bias, decay_log,
):
    value_width = value_pre.shape[1]
    x_conv = conv_silu(value_pre, value_kernel, value_bias, rim_rows[:, :value_width])
    bc_conv = conv_silu(state_pre, state_kernel, state_bias, rim_rows[:, value_width:])
    step_size = jax.nn.softplus(step_pre + step_bias)
    log_decay = -step_size * jnp.exp(decay_log)
    return x_conv, bc_conv, step_size, log_decay


def chain(decay, states, way):
    factor = jnp.ones_like(decay)
    total = from_behind(states, "row", way)
    for by in range(1, lax.axis_size("row") - 1):
        factor = factor * from_behind(decay, "row", way * by)
        piece = from_behind(states, "row", way * (by + 1))
        total = total + jnp.repeat(factor, HEADDIM)[:, None] * piece
    return total


def butterfly(part, axis):
    peers = lax.axis_size(axis)
    by = 1
    while by < peers:
        part = part + lax.ppermute(part, axis, [(i, i ^ by) for i in range(peers)])
        by *= 2
    return part


def halves_in(part, axis):
    peers, me = lax.axis_size(axis), lax.axis_index(axis)
    by = 1
    while by < peers:
        odd = (me // by) % 2 == 1
        half = part.shape[0] // 2
        first, second = part[:half], part[half:]
        given = lax.ppermute(
            jnp.where(odd, first, second), axis, [(i, i ^ by) for i in range(peers)]
        )
        part = jnp.where(odd, second, first) + given
        by *= 2
    return part


def halves_out(part, axis):
    peers, me = lax.axis_size(axis), lax.axis_index(axis)
    by = peers // 2
    while by >= 1:
        odd = (me // by) % 2 == 1
        given = lax.ppermute(part, axis, [(i, i ^ by) for i in range(peers)])
        part = jnp.concatenate([jnp.where(odd, given, part), jnp.where(odd, part, given)], axis=0)
        by //= 2
    return part


def right_product(grad_low, full_weight):
    return lax.dot_general(grad_low, full_weight, NT, preferred_element_type=jnp.float32)


def left_product(normed, grad_low):
    return lax.dot_general(normed, grad_low, TN, preferred_element_type=jnp.float32)


def from_col(part):
    return lax.ppermute(part, "col", [(0, 1), (1, 0)])


def col_sum(part):
    return part + from_col(part)


def body(
    layer_input,
    norm_gain,
    gate_weight,
    value_weight,
    state_weight,
    step_weight,
    value_kernel,
    value_bias,
    state_kernel,
    state_bias,
    step_bias,
    decay_log,
    skip_gain,
    gate_gain,
    out_weight,
    out_grad,
):
    value_width, state_width = value_weight.shape[1], state_weight.shape[1]
    head_part = step_weight.shape[1]
    scan_weights = lax.all_gather(
        jnp.concatenate([value_weight, state_weight, step_weight], axis=1), "row", axis=0, tiled=True
    )
    edge_weights = lax.all_gather(
        jnp.concatenate([gate_weight, out_weight], axis=1), "row", axis=0, tiled=True
    )
    gate_full, out_full = edge_weights[:, :value_width], edge_weights[:, value_width:]
    source = layer_input.astype(jnp.float32)
    scale_in = rms_scale(source)
    normed = (source * scale_in * norm_gain).astype(jnp.bfloat16)
    scan_pre = jnp.dot(normed, scan_weights, preferred_element_type=jnp.float32)
    wide = value_width + state_width
    value_pre, state_pre, step_pre = (
        scan_pre[:, :value_width], scan_pre[:, value_width:wide], scan_pre[:, wide:],
    )
    amount = normed.shape[0]
    margin = CONV - 1
    keep_prev = jnp.where(lax.axis_index("row") == 0, 0.0, 1.0).astype(jnp.float32)
    rim_rows = from_behind(scan_pre[amount - margin :, :wide], "row", 1) * keep_prev
    (x_conv, bc_conv, step_size, log_decay), ingredients_back = jax.vjp(
        ingredients, value_pre, state_pre, step_pre, rim_rows,
        value_kernel, value_bias, state_kernel, state_bias, step_bias, decay_log,
    )
    state_shape = (value_width, STATE)
    cumulative, end_state = chunk_call(
        end_state_kernel, head_part, amount, ("wide", "head", "head", "bc"), ("head", "state")
    )(x_conv, step_size, log_decay, bc_conv)
    decay_dev = jnp.exp(jnp.sum(log_decay, axis=0))
    gate_pre = jnp.dot(normed, gate_full, preferred_element_type=jnp.float32)
    cumulative_t = cumulative.T
    entry = chain(decay_dev, end_state, 1)
    y_scan, states = chunk_call(
        forward_kernel, head_part, amount,
        ("wide", "head", "head", "headt", "bc", "state"), ("wide", "states"),
        scratch=(state_shape,),
    )(x_conv, step_size, cumulative, cumulative_t, bc_conv, entry)
    skip = jnp.repeat(skip_gain, HEADDIM)
    y_flat = y_scan + skip * x_conv
    grad_mixed = jnp.dot(out_grad, out_full, preferred_element_type=jnp.float32)
    sigmoid_gate = jax.nn.sigmoid(gate_pre)
    gate_act = gate_pre * sigmoid_gate
    gated = y_flat * gate_act
    gained = grad_mixed * gate_gain
    sums = col_sum(
        jnp.stack([jnp.sum(gated * gated, axis=1), jnp.sum(gained * gated, axis=1)])
    )
    gate_scale = lax.rsqrt(sums[0] / INNER + EPSILON)[:, None]
    gate_inner = sums[1][:, None] / INNER
    grad_gated = gate_scale * gained - gated * gate_scale**3 * gate_inner
    grad_y = grad_gated * gate_act
    (grad_entry,) = chunk_call(
        entry_grad_kernel, head_part, amount, ("wide", "head", "bc"), ("state",), backward=True
    )(grad_y, cumulative, bc_conv)
    mixed_low = (gated * gate_scale * gate_gain).astype(jnp.bfloat16)
    partial_out = right_product(mixed_low, out_full)
    other_out = from_col(partial_out)
    grad_gate_pre = grad_gated * y_flat * sigmoid_gate * (1.0 + gate_pre * (1.0 - sigmoid_gate))
    gate_low = grad_gate_pre.astype(jnp.bfloat16)
    early_part = jnp.concatenate(
        [left_product(out_grad, mixed_low), left_product(normed, gate_low)], axis=1
    )
    gate_gain_part = jnp.sum(grad_mixed * gated * gate_scale, axis=0)
    skip_part = jnp.sum((x_conv * grad_y).reshape(amount, head_part, HEADDIM), axis=(0, 2))
    later_grad = chain(decay_dev, grad_entry, -1)
    early_part, later_grad = lax.optimization_barrier((early_part, later_grad))
    early = lax.psum_scatter(early_part, "row", scatter_dimension=0, tiled=True)
    grad_x, grad_bc, grad_step_size, grad_log_decay = chunk_call(
        backward_kernel, head_part, amount,
        ("wide", "head", "head", "headt", "bc", "wide", "wide", "states", "state"),
        ("wide", "bc", "head", "head"),
        backward=True, scratch=(state_shape, (SPAN, SPAN)), flops=16384,
    )(x_conv, step_size, cumulative, cumulative_t, bc_conv, grad_y, y_scan, states, later_grad)
    (
        grad_value_pre, grad_state_pre, grad_step_pre, grad_rim,
        grad_value_kernel, grad_value_bias, grad_state_kernel, grad_state_bias,
        grad_step_bias, grad_decay_log,
    ) = ingredients_back((grad_x + skip * grad_y, grad_bc, grad_step_size, grad_log_decay))
    from_next = from_behind(grad_rim * keep_prev, "row", -1)
    grad_scan_pre = jnp.concatenate([grad_value_pre, grad_state_pre, grad_step_pre], axis=1)
    from_next = jnp.pad(from_next, ((amount - margin, 0), (0, head_part)))
    scan_low = (grad_scan_pre + from_next).astype(jnp.bfloat16)
    scan_low, early = lax.optimization_barrier((scan_low, early))
    early = halves_in(early, "dp")
    grad_normed_part = right_product(gate_low, gate_full) + right_product(scan_low, scan_weights)
    grad_normed_part, other_out = lax.optimization_barrier((grad_normed_part, other_out))
    mixed_out = (source + (partial_out + other_out)).astype(jnp.bfloat16)
    other_grad = from_col(grad_normed_part)
    late = lax.psum_scatter(
        left_product(normed, scan_low), "row", scatter_dimension=0, tiled=True
    )
    late, early = lax.optimization_barrier((late, early))
    early = halves_out(early, "dp")
    late = halves_out(halves_in(late, "dp"), "dp")
    late, other_grad = lax.optimization_barrier((late, other_grad))
    late_state = col_sum(late[:, value_width:wide])
    grad_normed = grad_normed_part + other_grad
    gained_in = grad_normed * norm_gain
    input_inner = jnp.sum(gained_in * source, axis=1, keepdims=True)
    input_grad = (
        out_grad.astype(jnp.float32)
        + scale_in * gained_in
        - source * scale_in**3 * (input_inner / D)
    )
    norm_gain_part = jnp.sum(grad_normed_part * source * scale_in, axis=0)
    shared = (norm_gain_part, grad_state_kernel, grad_state_bias)
    own = (
        grad_value_kernel, grad_value_bias, grad_step_bias, grad_decay_log, skip_part,
        gate_gain_part,
    )
    own_flat = jnp.concatenate([part.reshape(-1) for part in own])
    col = lax.axis_index("col")
    own_slots = [jnp.where(col == i, own_flat, 0.0) for i in range(lax.axis_size("col"))]
    flat = jnp.concatenate([part.reshape(-1) for part in shared] + own_slots)
    for axis in ("row", "col", "dp"):
        flat = butterfly(flat, axis)

    def take(flat, parts):
        out, start = [], 0
        for part in parts:
            out.append(flat[start : start + part.size].reshape(part.shape))
            start += part.size
        return out

    shared_size = sum(part.size for part in shared)
    norm_gain_grad, grad_state_kernel, grad_state_bias = take(flat[:shared_size], shared)
    (
        grad_value_kernel, grad_value_bias, grad_step_bias, grad_decay_log, grad_skip_gain,
        gate_gain_grad,
    ) = take(
        lax.dynamic_slice_in_dim(flat, shared_size + col * own_flat.size, own_flat.size), own
    )
    return (
        mixed_out,
        input_grad,
        norm_gain_grad,
        early[:, value_width:],
        late[:, :value_width],
        late_state,
        late[:, wide:],
        grad_value_kernel,
        grad_value_bias,
        grad_state_kernel,
        grad_state_bias,
        grad_step_bias,
        grad_decay_log,
        grad_skip_gain,
        gate_gain_grad,
        early[:, :value_width],
    )


def solution(mesh):
    in_specs = (
        P(("dp", "row"), None),
        P(),
        P("row", "col"),
        P("row", "col"),
        P("row", None),
        P("row", "col"),
        P(None, "col"),
        P("col"),
        P(),
        P(),
        P("col"),
        P("col"),
        P("col"),
        P("col"),
        P("row", "col"),
        P(("dp", "row"), None),
    )
    out_specs = (
        P(("dp", "row"), None),
        P(("dp", "row"), None),
        P(),
        P("row", "col"),
        P("row", "col"),
        P("row", None),
        P("row", "col"),
        P(None, "col"),
        P("col"),
        P(),
        P(),
        P("col"),
        P("col"),
        P("col"),
        P("col"),
        P("row", "col"),
    )
    return jax.shard_map(body, mesh=mesh, in_specs=in_specs, out_specs=out_specs, check_vma=False)
```
